128 devices in a mesh: stn: 32 (over y_lo, z, x), tm: 4 (over y_hi, core).
Axes of the slice: x: 4, y: 4 (y_hi: 2, y_lo: 2; y = y_hi * 2 + y_lo), z: 4, core: 2. Of those that a mesh axis runs over, the one named last changes fastest.
Arguments:
- voltages: bfloat16 [512, 4, 11, 2048], P('stn', 'tm'), may hold values from -6 to 6
- pfb_taps: float32 [4, 2048], replicated, may hold values from -3 to 3
- grid_kernel: float32 [8, 8], replicated, may hold values from 0.25 to 1
- uv_corners: int32 [32, 4, 34, 2, 256], P('stn', 'tm'), may hold values from 0 to 24
- kernel_offsets: int32 [32, 4, 34, 2, 256], P('stn', 'tm'), may hold values from 0 to 7
- row_counts: int32 [32, 4, 34], P('stn', 'tm'), may hold values from 128 to 256, as said below
- grid_tiles: int32 [32, 4, 34], P('stn', 'tm'), may hold values from 0 to 31, as said below
Outputs:
- uv_grid: float32 [32, 1024, 8, 256], P('stn', None, 'tm')
The draws below stay inside these ranges and needn't reach their ends.
Inputs may be any that keep to these rules, and one draw needn't show every extreme that they name: `uv_corners`: each tile's kernel footprint of 8 cells along each direction lies inside its grid tile of 32 cells. `row_counts`: rows of a tile at or beyond its count are flagged. Every group and channel share has a tile with all 256 rows live and a tile with half of them live. `grid_tiles`: at most 2 tiles of one group and channel share name the same grid tile; in every draw some grid tile is named exactly 2 times by every group and channel share.
All inputs are finite; a program needn't handle non-finite values.
Results may differ from the reference program's by a relative error of at most 0.0072.
Values may be sent and summed in bfloat16 or wider, within the bound.
A program may use at most 128 MiB of HBM per device.

```python
import math
import jax
import jax.numpy as jnp
from jax import lax

STN_DEV = 16
CHANNELS = 1024
FRAME = 2048
TAPS = 4
FR_DEV = 8
FRAMES = 32
STATIONS = 512
BLOCK_CH = 128
CH_BLOCKS = 2
OFFSETS = 17
TILES_DEV = 34
ROWS = 256
SIDE = 32
CELLS = 1024
SUPPORT = 8
OVERSAMPLE = 8
MOST = 2
GRID_TILES = 32
N_STN = 32
N_TM = 4


def draw_grid_tiles(key, part):
    key = jax.random.fold_in(key, 11)
    key_hot, key_bias, key_noise, key_order = jax.random.split(key, 4)
    hot_tile = jax.random.randint(key_hot, (), 0, N_STN)
    popular = jax.random.randint(key_bias, (N_STN,), 0, 8192)
    candidates = N_STN * MOST
    owner_of = jnp.arange(candidates, dtype=jnp.int32) // MOST
    noise_int = jax.random.randint(key_noise, (N_STN, N_TM, candidates), 0, 4096)
    scores = (noise_int + popular[owner_of][None, None, :]) * candidates + jnp.arange(candidates, dtype=jnp.int32)[None, None, :]
    scores = jnp.where(owner_of[None, None, :] == hot_tile, -1, scores)
    unused_vals, picked = lax.top_k(scores, TILES_DEV - MOST)
    chosen = owner_of[picked]
    hot_rows = jnp.zeros((N_STN, N_TM, MOST), jnp.int32) + hot_tile
    tiles_all = jnp.concatenate([hot_rows, chosen], axis=2)
    order_key = jax.random.randint(key_order, (N_STN, N_TM, TILES_DEV), 0, 65536) * TILES_DEV + jnp.arange(TILES_DEV, dtype=jnp.int32)[None, None, :]
    order_idx = jnp.argsort(order_key, axis=2)
    return jnp.take_along_axis(tiles_all, order_idx, axis=2).astype(jnp.int32)


def draw_row_counts(key, part):
    key = jax.random.fold_in(key, 23)
    key_base, key_full, key_half = jax.random.split(key, 3)
    counts = ROWS // 2 + jax.random.randint(key_base, (N_STN, N_TM, TILES_DEV), 0, ROWS // 2 + 1)
    full_at = jax.random.randint(key_full, (N_STN, N_TM, 1), 0, TILES_DEV)
    half_at = (full_at + 1 + jax.random.randint(key_half, (N_STN, N_TM, 1), 0, TILES_DEV - 1)) % TILES_DEV
    index_ids = jnp.arange(TILES_DEV, dtype=jnp.int32)[None, None, :]
    counts = jnp.where(index_ids == full_at, ROWS, counts)
    counts = jnp.where(index_ids == half_at, ROWS // 2, counts)
    return counts.astype(jnp.int32)


def set_ends(drawn, own_key, smallest, high):
    longest = drawn.shape.index(max(drawn.shape))
    spots = []
    for shift in (0, 1):
        where = [jax.random.randint(jax.random.fold_in(own_key, axis), (), 0, length) for axis, length in enumerate(drawn.shape)]
        where[longest] = (where[longest] + shift) % drawn.shape[longest]
        spots.append(tuple(where))
    return drawn.at[spots[0]].set(smallest).at[spots[1]].set(high)


def block_levels(own_key, dims, cuts, least, largest):
    def one(axis_at, blocks):
        draws = jax.random.uniform(jax.random.fold_in(jax.random.fold_in(own_key, 6), axis_at), (blocks,), jnp.float32, least / len(cuts), largest / len(cuts))
        return jnp.repeat(jnp.exp(draws), dims[axis_at] // blocks).reshape((-1,) + (1,) * (len(dims) - axis_at - 1))

    factor_of = one(*cuts[0])
    for cut in cuts[1:]:
        factor_of = factor_of * one(*cut)
    return factor_of


def noise(key, shape, deviation, bound, cuts=(), held_as=jnp.bfloat16):
    gain = block_levels(key, shape, cuts, -0.22, 0.18) if cuts else 1.0
    entries = jax.random.normal(key, shape, jnp.float32) * deviation * gain
    return jnp.minimum(jnp.maximum(entries, -bound), bound).astype(held_as)


def setup_inputs(seed: int = 0) -> dict:
    arg_keys = jax.random.split(jax.random.key(seed), 8)
    voltages = noise(arg_keys[0], (STATIONS, N_TM, FR_DEV + TAPS - 1, FRAME), 1.0, 6.0, ((0, 32), (1, 4)))
    pfb_taps = noise(arg_keys[1], (TAPS, FRAME), 0.5, 3.0, (), jnp.float32)
    grid_kernel = jnp.clip(jax.random.uniform(arg_keys[2], (OVERSAMPLE, SUPPORT), jnp.float32, 0.25, 1.0), 0.25, 1.0)
    uv_corners = set_ends(jax.random.randint(arg_keys[3], (N_STN, N_TM, TILES_DEV, 2, ROWS), 0, SIDE - SUPPORT + 1), jax.random.fold_in(arg_keys[3], 1), 0, SIDE - SUPPORT).astype(jnp.int32)
    kernel_offsets = set_ends(jax.random.randint(arg_keys[4], (N_STN, N_TM, TILES_DEV, 2, ROWS), 0, OVERSAMPLE), jax.random.fold_in(arg_keys[4], 1), 0, OVERSAMPLE - 1).astype(jnp.int32)
    row_counts = draw_row_counts(jax.random.fold_in(arg_keys[7], 71), 0)
    grid_tiles = draw_grid_tiles(jax.random.fold_in(arg_keys[7], 71), 0)
    return {"voltages": voltages, "pfb_taps": pfb_taps, "grid_kernel": grid_kernel, "uv_corners": uv_corners, "kernel_offsets": kernel_offsets, "row_counts": row_counts, "grid_tiles": grid_tiles}


def polyphase(voltages, filter_taps):
    frames = voltages.shape[1] - TAPS + 1
    filtered = jnp.zeros((voltages.shape[0], frames, voltages.shape[2]), jnp.float32)
    for tap_index in range(TAPS):
        filtered = filtered + filter_taps[tap_index][None, None, :] * voltages[:, tap_index:tap_index + frames, :].astype(jnp.float32)
    return filtered.astype(jnp.bfloat16)

def transform_block(first_chan, block_width):
    samples = jnp.arange(FRAME, dtype=jnp.int32)
    channel_ids = first_chan + jnp.arange(block_width, dtype=jnp.int32)
    phase_int = samples[:, None] * channel_ids[None, :] % FRAME
    angle_rad = phase_int.astype(jnp.float32) * (2.0 * math.pi / FRAME)
    norm_scale = 1.0 / math.sqrt(FRAME)
    return ((jnp.cos(angle_rad) * norm_scale).astype(jnp.bfloat16), (-jnp.sin(angle_rad) * norm_scale).astype(jnp.bfloat16))

def correlate(local_block, other_block):
    frames = local_block.shape[1]
    product = jnp.einsum('atpc,btqc->cpaqb', local_block.astype(jnp.float32), other_block.astype(jnp.float32))
    real_part = product[:, 0, :, 0, :] + product[:, 1, :, 1, :]
    imag_part = product[:, 1, :, 0, :] - product[:, 0, :, 1, :]
    visibility = jnp.stack([real_part, imag_part], axis=1) * (1.0 / frames)
    chan_count = visibility.shape[0]
    visibility = visibility.reshape(chan_count // BLOCK_CH, BLOCK_CH, 2, ROWS)
    visibility = jnp.transpose(visibility, (0, 3, 2, 1))
    return visibility.reshape(chan_count // BLOCK_CH, ROWS, 2 * BLOCK_CH).astype(jnp.bfloat16)

def tile_weights(corners, offsets, row_count, kernel):
    choose = offsets[:, :, None] == jnp.arange(kernel.shape[0], dtype=jnp.int32)[None, None, :]
    kern_rows = lax.optimization_barrier(jnp.sum(jnp.where(choose[:, :, :, None], kernel[None, None, :, :], 0.0), axis=2))
    places = jnp.arange(SIDE, dtype=jnp.int32)
    reach_at = jnp.arange(kernel.shape[1], dtype=jnp.int32)
    hit_mask = places[None, None, :, None] == corners[:, :, None, None] + reach_at[None, None, None, :]
    axis_weight = lax.optimization_barrier(jnp.sum(jnp.where(hit_mask, kern_rows[:, :, None, :], 0.0), axis=3))
    live_rows = (jnp.arange(corners.shape[1], dtype=jnp.int32) < row_count).astype(jnp.float32)
    weights = axis_weight[1][:, :, None] * axis_weight[0][:, None, :] * live_rows[:, None, None]
    return weights.reshape(corners.shape[1], SIDE * SIDE).astype(jnp.bfloat16)

def reference(voltages, pfb_taps, grid_kernel, uv_corners, kernel_offsets, row_counts, grid_tiles):
    filtered = polyphase(voltages.reshape(STATIONS * N_TM, FR_DEV + TAPS - 1, FRAME), pfb_taps)
    cos_part, sin_part = transform_block(0, CHANNELS)
    dft_table = jnp.concatenate([cos_part, sin_part], axis=1).astype(jnp.float32)
    spectra = jnp.dot(filtered.reshape(-1, FRAME).astype(jnp.float32), dft_table)
    spectra = spectra.astype(jnp.bfloat16).reshape(STATIONS, FRAMES, 2, CHANNELS)
    lists_all = jnp.concatenate([uv_corners, kernel_offsets], axis=3)
    tile_total = N_TM * TILES_DEV
    tile_index = jnp.arange(tile_total, dtype=jnp.int32)
    global_block = tile_index // TILES_DEV * CH_BLOCKS + tile_index % CH_BLOCKS

    def per_group(group_id, grid_sum):
        group_id = jnp.asarray(group_id).astype(jnp.int32)
        local_block = lax.dynamic_slice_in_dim(spectra, group_id * STN_DEV, STN_DEV, 0)
        stacked = []
        for offset_id in range(OFFSETS):
            partner = ((group_id + offset_id) % N_STN).astype(jnp.int32)
            other_block = lax.dynamic_slice_in_dim(spectra, partner * STN_DEV, STN_DEV, 0)
            stacked.append(correlate(local_block, other_block))
        vis_all = jnp.stack(stacked).reshape(OFFSETS, N_TM, CH_BLOCKS, ROWS, 2 * BLOCK_CH)
        vis_all = jnp.transpose(vis_all, (1, 0, 2, 3, 4)).reshape(tile_total, ROWS, 2 * BLOCK_CH)
        group_lists = lists_all[group_id].reshape(tile_total, 4, ROWS)
        counts = row_counts[group_id].reshape(-1)
        weights = jax.vmap(tile_weights, (0, 0, 0, None))(group_lists[:, :2], group_lists[:, 2:], counts, grid_kernel)
        slot_terms = jnp.einsum('nrx,nrc->nxc', weights.astype(jnp.float32), vis_all.astype(jnp.float32))
        targets = grid_tiles[group_id].reshape(-1)
        return grid_sum.at[targets, :, global_block, :].add(slot_terms)
    grid_sum = jnp.zeros((GRID_TILES, CELLS, CHANNELS // BLOCK_CH, 2 * BLOCK_CH), jnp.float32)
    return lax.fori_loop(0, N_STN, per_group, grid_sum)
```

```python
import math

import jax
import jax.numpy as jnp
import ml_dtypes
import numpy as np
from jax import lax
from jax.experimental import pallas as pl
from jax.experimental.pallas import tpu as pltpu
from jax.sharding import PartitionSpec as P

CHANNELS = 1024
FRAME = 2048
TAPS = 4
FR_DEV = 8
STN_DEV = 16
BLOCK_CH = 128
ROWS = 256
SIDE = 32
CELLS = 1024
MOST = 2
GROUPS = 32
SLOTS = GROUPS * MOST
LISTS = 4 * ROWS
BF = jnp.bfloat16
F32 = jnp.float32
MESH = pl.DeviceIdType.MESH

UNITS = 32
A0, A1 = 0, 11
B0, B1 = 11, 22
C10, C1M, C11 = 22, 25, 27
C20, C2M, C21 = 27, 29, 32
MESSAGES = 38


def dft_table():
    samples = np.arange(FRAME, dtype=np.int64)
    channels = np.arange(CHANNELS, dtype=np.int64)
    phase = (samples[:, None] * channels[None, :]) % FRAME
    angle = phase.astype(np.float32) * np.float32(2.0 * math.pi / FRAME)
    scale = np.float32(1.0 / math.sqrt(FRAME))
    parts = np.stack([np.cos(angle) * scale, -np.sin(angle) * scale], axis=1)
    parts = parts.reshape(FRAME, 2, 4, 2, BLOCK_CH).transpose(2, 0, 3, 1, 4)
    return parts.reshape(4, FRAME, 4 * BLOCK_CH).astype(ml_dtypes.bfloat16)


def gather_kernel(info, filtered, table, out, grp0, grp1, grp2, grp3, held, tab, rows32, vis, tab_sem, a2a_send, a2a_recv, send_sem, recv_sem, out_sem):
    grp = (grp0, grp1, grp2, grp3)
    me_s = lax.axis_index("stn")
    me_t = lax.axis_index("tm")
    y, z, x = me_s // 16, (me_s // 4) % 4, me_s % 4
    xp, xm = (x + 1) % 4, (x + 3) % 4
    zp, zm = (z + 1) % 4, (z + 3) % 4
    yn = 1 - y

    def at(yy, zz, xx):
        return yy * 16 + zz * 4 + xx

    to = {
        "xp": at(y, z, xp),
        "xm": at(y, z, xm),
        "zp": at(y, zp, x),
        "zm": at(y, zm, x),
        "y": at(yn, z, x),
    }
    chunk = [(me_t + k) % 4 for k in range(4)]

    table_copies = [
        pltpu.make_async_copy(table.at[chunk[k]], tab.at[k], tab_sem.at[k]) for k in range(4)
    ]
    for copy in table_copies:
        copy.start()

    barrier = pltpu.get_barrier_semaphore()
    for name in to:
        pl.semaphore_signal(barrier, inc=1, device_id={"stn": to[name]}, device_id_type=MESH)
    for k in range(1, 4):
        pl.semaphore_signal(barrier, inc=1, device_id={"tm": chunk[k]}, device_id_type=MESH)

    def message(k, number, where, dest):
        ref = grp[k].at[where]
        return pltpu.make_async_remote_copy(
            src_ref=ref,
            dst_ref=ref,
            send_sem=send_sem.at[k, number],
            recv_sem=recv_sem.at[k, number],
            device_id={"stn": to[dest]},
            device_id_type=MESH,
        )

    def span(lo, hi):
        return pl.ds(lo, hi - lo)

    full4 = pl.ds(0, 4)
    both = pl.ds(0, 2)

    def build(k):
        def msg(number, where, dest):
            return (number, message(k, number, where, dest))

        a, b = span(A0, A1), span(B0, B1)
        c1, c2, c = span(C10, C11), span(C20, C21), span(C10, C21)
        direct1 = [
            msg(1, (y, z, x, c1), "xp"),
            msg(2, (y, z, x, c1), "xm"),
            msg(5, (y, z, x, c2), "zp"),
            msg(6, (y, z, x, c2), "zm"),
            msg(0, (y, z, x, span(A0, B1)), "y"),
        ]
        fwd1 = [
            (1, msg(3, (y, z, xm, span(C10, C1M)), "xp")),
            (2, msg(4, (y, z, xp, span(C1M, C11)), "xm")),
            (5, msg(7, (y, zm, x, span(C20, C2M)), "zp")),
            (6, msg(8, (y, zp, x, span(C2M, C21)), "zm")),
        ]
        rest1 = [0, 3, 4, 7, 8]
        direct2 = [
            msg(9, (both, z, x, a), "xp"),
            msg(10, (both, z, x, a), "xm"),
            msg(13, (both, z, x, b), "zp"),
            msg(14, (both, z, x, b), "zm"),
            msg(17, (y, z, full4, c1), "zp"),
            msg(18, (y, z, full4, c1), "zm"),
            msg(21, (y, full4, x, c2), "xp"),
            msg(22, (y, full4, x, c2), "xm"),
        ]
        lo2, hi2 = pl.ds(0, 2), pl.ds(2, 2)
        fwd2 = [
            (9, msg(11, (0, z, xm, a), "xp")),
            (10, msg(12, (1, z, xp, a), "xm")),
            (13, msg(15, (0, zm, x, b), "zp")),
            (14, msg(16, (1, zp, x, b), "zm")),
            (17, msg(19, (y, zm, lo2, c1), "zp")),
            (18, msg(20, (y, zp, hi2, c1), "zm")),
            (21, msg(23, (y, lo2, xm, c2), "xp")),
            (22, msg(24, (y, hi2, xp, c2), "xm")),
        ]
        rest2 = [11, 12, 15, 16, 19, 20, 23, 24]
        direct3 = [
            msg(25, (0, z, full4, a), "zp"),
            msg(27, (1, z, full4, a), "zm"),
            msg(31, (0, full4, x, b), "xp"),
            msg(33, (1, full4, x, b), "xm"),
            msg(37, (y, full4, full4, c), "y"),
            msg(26, (1, z, full4, a), "zp"),
            msg(28, (0, z, full4, a), "zm"),
            msg(32, (1, full4, x, b), "xp"),
            msg(34, (0, full4, x, b), "xm"),
        ]
        fwd3 = [
            (25, msg(29, (0, zm, full4, a), "zp")),
            (27, msg(30, (1, zp, full4, a), "zm")),
            (31, msg(35, (0, full4, xm, b), "xp")),
            (33, msg(36, (1, full4, xp, b), "xm")),
        ]
        rest3 = [26, 28, 32, 34, 29, 30, 35, 36, 37]
        return {1: (direct1, fwd1, rest1), 2: (direct2, fwd2, rest2), 3: (direct3, fwd3, rest3)}

    plan = [build(k) for k in range(4)]
    by_number = []
    for k in range(4):
        found = {}
        for step in (1, 2, 3):
            direct, fwd, rest = plan[k][step]
            for number, copy in direct:
                found[number] = copy
            for unused, (number, copy) in fwd:
                found[number] = copy
        by_number.append(found)

    def direct(step, k):
        for unused, copy in plan[k][step][0]:
            copy.start()

    def forward(step, k):
        for arrived, (unused, copy) in plan[k][step][1]:
            by_number[k][arrived].wait_recv()
            copy.start()

    def finish(step, k):
        for number in plan[k][step][2]:
            by_number[k][number].wait_recv()

    def transform(k, store):
        table_copies[k].wait()
        spectra = jnp.dot(filtered[...], tab[k], preferred_element_type=F32).astype(BF)
        for m in range(2):
            for t in range(FR_DEV):
                for p in range(2):
                    column = (m * 2 + p) * BLOCK_CH
                    store(
                        m * 16 + t * 2 + p,
                        spectra[t * STN_DEV : (t + 1) * STN_DEV, column : column + BLOCK_CH],
                    )

    def store_own(unit, value):
        grp[0][y, z, x, unit] = value

    transform(0, store_own)
    pl.semaphore_wait(barrier, 8)
    direct(1, 0)

    exchange = []
    for k in range(1, 4):

        def store_held(unit, value, k=k):
            held[k - 1, unit] = value

        transform(k, store_held)
        copy = pltpu.make_async_remote_copy(
            src_ref=held.at[k - 1],
            dst_ref=grp[4 - k].at[y, z, x],
            send_sem=a2a_send.at[k],
            recv_sem=a2a_recv.at[k],
            device_id={"tm": chunk[k]},
            device_id_type=MESH,
        )
        copy.start()
        exchange.append(copy)

    def exchanged(k):
        pltpu.make_async_remote_copy(
            src_ref=held.at[0],
            dst_ref=grp[k].at[y, z, x],
            send_sem=a2a_send.at[4 - k],
            recv_sem=a2a_recv.at[4 - k],
            device_id={"tm": chunk[k]},
            device_id_type=MESH,
        ).wait_recv()

    def correlate(k, first, last):
        def slot(s, carry):
            g = s // MOST
            partner, m = info[s * 2], info[s * 2 + 1]
            units = pl.ds(m * 16, 16)
            own = grp[k][g // 16, (g // 4) % 4, g % 4, units]
            rows32[...] = own.reshape(256, BLOCK_CH).astype(F32)
            other = grp[k][partner // 16, (partner // 4) % 4, partner % 4, units]
            for a in range(STN_DEV):
                real, imag = [], []
                for t in range(FR_DEV):
                    r = t * 32 + a
                    a_r = jnp.broadcast_to(rows32[r : r + 1, :], (STN_DEV, BLOCK_CH)).astype(BF)
                    a_i = jnp.broadcast_to(
                        rows32[r + 16 : r + 17, :], (STN_DEV, BLOCK_CH)
                    ).astype(BF)
                    b_r, b_i = other[2 * t], other[2 * t + 1]
                    real += [a_r * b_r + a_i * b_i]
                    imag += [a_i * b_r - a_r * b_i]
                while len(real) > 1:
                    real = [real[i] + real[i + 1] for i in range(0, len(real), 2)]
                    imag = [imag[i] + imag[i + 1] for i in range(0, len(imag), 2)]
                rows = slice(a * STN_DEV, (a + 1) * STN_DEV)
                if k == 0:
                    vis[s, rows, :BLOCK_CH] = real[0]
                    vis[s, rows, BLOCK_CH:] = imag[0]
                else:
                    vis[s, rows, :BLOCK_CH] = vis[s, rows, :BLOCK_CH] + real[0]
                    vis[s, rows, BLOCK_CH:] = vis[s, rows, BLOCK_CH:] + imag[0]
            return carry

        lax.fori_loop(first, last, slot, 0)

    half = SLOTS // 2
    for stage in range(6):
        active = [(step, stage - step + 1) for step in (3, 2, 1) if 0 <= stage - step + 1 < 4]
        for step, k in active:
            if step == 1 and k == 0:
                continue
            if step == 1:
                exchanged(k)
            direct(step, k)
        if stage >= 3:
            correlate(stage - 3, 0, half)
        for step, k in active:
            forward(step, k)
        if stage >= 3:
            correlate(stage - 3, half, SLOTS)
        for step, k in active:
            finish(step, k)
    copies = []
    for i in range(4):
        part = pl.ds(i * (SLOTS // 4), SLOTS // 4)
        correlate(3, i * (SLOTS // 4), (i + 1) * (SLOTS // 4))
        copy = pltpu.make_async_copy(vis.at[part], out.at[part], out_sem.at[i])
        copy.start()
        copies.append(copy)
    for k in range(4):
        for number in range(MESSAGES):
            by_number[k][number].wait_send()
    for copy in exchange:
        copy.wait_send()
    for copy in copies:
        copy.wait()


def gather_and_correlate(info, filtered, table):
    return pl.pallas_call(
        gather_kernel,
        out_shape=jax.ShapeDtypeStruct((SLOTS, ROWS, 2 * BLOCK_CH), BF),
        in_specs=[
            pl.BlockSpec(memory_space=pltpu.SMEM),
            pl.BlockSpec(memory_space=pltpu.VMEM),
            pl.BlockSpec(memory_space=pl.ANY),
        ],
        out_specs=pl.BlockSpec(memory_space=pl.ANY),
        scratch_shapes=[
            *[pltpu.VMEM((2, 4, 4, UNITS, STN_DEV, BLOCK_CH), BF) for unused in range(4)],
            pltpu.VMEM((3, UNITS, STN_DEV, BLOCK_CH), BF),
            pltpu.VMEM((4, FRAME, 4 * BLOCK_CH), BF),
            pltpu.VMEM((256, BLOCK_CH), F32),
            pltpu.VMEM((SLOTS, ROWS, 2 * BLOCK_CH), BF),
            pltpu.SemaphoreType.DMA((4,)),
            pltpu.SemaphoreType.DMA((4,)),
            pltpu.SemaphoreType.DMA((4,)),
            pltpu.SemaphoreType.DMA((4, MESSAGES)),
            pltpu.SemaphoreType.DMA((4, MESSAGES)),
            pltpu.SemaphoreType.DMA((4,)),
        ],
        compiler_params=pltpu.CompilerParams(
            collective_id=0, has_side_effects=True, vmem_limit_bytes=48 * 2**20
        ),
        name="gather_correlate",
    )(info, filtered, table)


def grid_kernel_body(info, count, lists, kernel_t, vis, out, total, weights):
    total[...] = jnp.zeros_like(total)

    def axis_weight(position, offset):
        chosen = jnp.zeros((8, ROWS), F32)
        for o in range(8):
            column = jnp.broadcast_to(kernel_t[:, o : o + 1], (8, ROWS))
            chosen = jnp.where(jnp.broadcast_to(offset == o, (8, ROWS)), column, chosen)
        reach = lax.broadcasted_iota(jnp.int32, (SIDE, ROWS), 0) - jnp.broadcast_to(
            position, (SIDE, ROWS)
        )
        placed = jnp.zeros((SIDE, ROWS), F32)
        for k in range(8):
            placed = jnp.where(
                reach == k, jnp.broadcast_to(chosen[k : k + 1], (SIDE, ROWS)), placed
            )
        return placed

    def slot(s, carry):
        m = info[s * 2 + 1]
        rows = lists[s].astype(jnp.int32)
        along_x = axis_weight(rows[0:1], rows[2:3])
        along_y = axis_weight(rows[1:2], rows[3:4])
        live = lax.broadcasted_iota(jnp.int32, (SIDE, ROWS), 1) < count[s]
        along_y = jnp.where(live, along_y, 0.0)
        for v in range(SIDE):
            weights[v * SIDE : (v + 1) * SIDE] = (
                along_x * jnp.broadcast_to(along_y[v : v + 1], (SIDE, ROWS))
            ).astype(BF)
        total[m] += jnp.dot(weights[...], vis[s], preferred_element_type=F32)
        return carry

    lax.fori_loop(0, SLOTS, slot, 0)
    for m in range(2):
        out[:, m * 256 : (m + 1) * 256] = total[m] * (1.0 / 32.0)


def gridding(info, count, lists, kernel_t, vis):
    vmem = pl.BlockSpec(memory_space=pltpu.VMEM)
    smem = pl.BlockSpec(memory_space=pltpu.SMEM)
    return pl.pallas_call(
        grid_kernel_body,
        out_shape=jax.ShapeDtypeStruct((CELLS, 2 * 2 * BLOCK_CH), F32),
        in_specs=[smem, smem, vmem, vmem, vmem],
        out_specs=vmem,
        scratch_shapes=[
            pltpu.VMEM((2, CELLS, 2 * BLOCK_CH), F32),
            pltpu.VMEM((CELLS, ROWS), BF),
        ],
        compiler_params=pltpu.CompilerParams(vmem_limit_bytes=40 * 2**20),
        name="gridding",
    )(info, count, lists, kernel_t, vis)


def polyphase(voltages, filter_taps):
    by_frame = jnp.transpose(voltages, (1, 0, 2))
    frames = by_frame.shape[0] - TAPS + 1
    filtered = jnp.zeros((frames,) + by_frame.shape[1:], F32)
    for tap in range(TAPS):
        filtered = filtered + filter_taps[tap][None, None, :] * by_frame[
            tap : tap + frames
        ].astype(F32)
    return filtered.astype(BF).reshape(frames * by_frame.shape[1], FRAME)


def route(uv_corners, kernel_offsets, row_counts, grid_tiles):
    owners = grid_tiles[0, 0]
    tiles = owners.shape[0]
    tile_ids = jnp.arange(tiles, dtype=jnp.int32)
    extra = jnp.stack([row_counts[0, 0], tile_ids // 2, tile_ids % 2], axis=1)
    extra = jnp.pad(extra, ((0, 0), (0, 125)))
    packed = jnp.concatenate(
        [uv_corners[0, 0].reshape(tiles, 512), kernel_offsets[0, 0].reshape(tiles, 512), extra],
        axis=1,
    ).astype(BF)
    same = owners[:, None] == owners[None, :]
    earlier = tile_ids[None, :] < tile_ids[:, None]
    slot_of = jnp.sum((same & earlier).astype(jnp.int32), axis=1)
    target = owners * MOST + slot_of
    picker = (target[None, :] == jnp.arange(SLOTS, dtype=jnp.int32)[:, None]).astype(BF)
    send = jnp.dot(picker, packed, preferred_element_type=F32).astype(BF)
    send = send.reshape(GROUPS, MOST, LISTS + 128)
    got = lax.all_to_all(send, "stn", split_axis=0, concat_axis=0, tiled=True)
    got = got.reshape(SLOTS, LISTS + 128)
    facts = got[:, LISTS : LISTS + 3].astype(jnp.int32)
    group = jnp.arange(SLOTS, dtype=jnp.int32) // MOST
    partner = (group + facts[:, 1]) % GROUPS
    info = jnp.stack([partner, facts[:, 2]], axis=1).reshape(-1)
    return info, facts[:, 0], got[:, :LISTS].reshape(SLOTS, 4, ROWS).astype(F32)


def on_device(voltages, pfb_taps, grid_kernel, uv_corners, kernel_offsets, row_counts, grid_tiles):
    info, count, lists = route(uv_corners, kernel_offsets, row_counts, grid_tiles)
    filtered = polyphase(voltages[:, 0], pfb_taps)
    vis = gather_and_correlate(info, filtered, jnp.asarray(dft_table()))
    gridded = gridding(info, count, lists, grid_kernel.T, vis)
    return gridded.reshape(1, CELLS, 2, 2 * BLOCK_CH)


def solution(mesh):
    return jax.shard_map(
        on_device,
        mesh=mesh,
        in_specs=(
            P("stn", "tm", None, None),
            P(),
            P(),
            P("stn", "tm", None, None, None),
            P("stn", "tm", None, None, None),
            P("stn", "tm", None),
            P("stn", "tm", None),
        ),
        out_specs=P("stn", None, "tm", None),
        check_vma=False,
    )
```

```python
import math

import jax
import jax.numpy as jnp
import ml_dtypes
import numpy as np
from jax import lax
from jax.experimental import pallas as pl
from jax.experimental.pallas import tpu as pltpu
from jax.sharding import PartitionSpec as P

CHANNELS = 1024
FRAME = 2048
TAPS = 4
FR_DEV = 8
STN_DEV = 16
BLOCK_CH = 128
ROWS = 256
SIDE = 32
CELLS = 1024
MOST = 2
GROUPS = 32
SLOTS = GROUPS * MOST
LISTS = 4 * ROWS
BF = jnp.bfloat16
F32 = jnp.float32
MESH = pl.DeviceIdType.MESH

UNITS = 32
A0, A1 = 0, 11
B0, B1 = 11, 22
C10, C1M, C11 = 22, 25, 27
C20, C2M, C21 = 27, 29, 32
MESSAGES = 38


def dft_table():
    samples = np.arange(FRAME, dtype=np.int64)
    channels = np.arange(CHANNELS, dtype=np.int64)
    phase = (samples[:, None] * channels[None, :]) % FRAME
    angle = phase.astype(np.float32) * np.float32(2.0 * math.pi / FRAME)
    scale = np.float32(1.0 / math.sqrt(FRAME))
    parts = np.stack([np.cos(angle) * scale, -np.sin(angle) * scale], axis=1)
    parts = parts.reshape(FRAME, 2, 4, 2, BLOCK_CH).transpose(2, 0, 3, 1, 4)
    return parts.reshape(4, FRAME, 4 * BLOCK_CH).astype(ml_dtypes.bfloat16)


def gather_kernel(
    lists,
    facts,
    filtered,
    table,
    out,
    out_lists,
    out_facts,
    grp0,
    grp1,
    grp2,
    grp3,
    held,
    tab,
    rows32,
    vis,
    to_send,
    by_y,
    by_z,
    by_x,
    facts_all,
    info,
    tab_sem,
    a2a_send,
    a2a_recv,
    send_sem,
    recv_sem,
    out_sem,
    route_send,
    route_recv,
    own_sem,
):
    grp = (grp0, grp1, grp2, grp3)
    me_s = lax.axis_index("stn")
    me_t = lax.axis_index("tm")
    y, z, x = me_s // 16, (me_s // 4) % 4, me_s % 4
    xp, xm = (x + 1) % 4, (x + 3) % 4
    zp, zm = (z + 1) % 4, (z + 3) % 4
    yn = 1 - y

    def at(yy, zz, xx):
        return yy * 16 + zz * 4 + xx

    to = {
        "xp": at(y, z, xp),
        "xm": at(y, z, xm),
        "zp": at(y, zp, x),
        "zm": at(y, zm, x),
        "y": at(yn, z, x),
    }
    along_z = [at(y, (z + i) % 4, x) for i in range(4)]
    along_x = [at(y, z, (x + i) % 4) for i in range(4)]
    chunk = [(me_t + k) % 4 for k in range(4)]

    table_copies = [
        pltpu.make_async_copy(table.at[chunk[k]], tab.at[k], tab_sem.at[k]) for k in range(4)
    ]
    table_copies[0].start()

    barrier = pltpu.get_barrier_semaphore()
    for name in to:
        pl.semaphore_signal(barrier, inc=1, device_id={"stn": to[name]}, device_id_type=MESH)
    for far in (along_z[2], along_x[2]):
        pl.semaphore_signal(barrier, inc=1, device_id={"stn": far}, device_id_type=MESH)
    for k in range(1, 4):
        pl.semaphore_signal(barrier, inc=1, device_id={"tm": chunk[k]}, device_id_type=MESH)

    def message(k, number, where, dest):
        ref = grp[k].at[where]
        return pltpu.make_async_remote_copy(
            src_ref=ref,
            dst_ref=ref,
            send_sem=send_sem.at[k, number],
            recv_sem=recv_sem.at[k, number],
            device_id={"stn": to[dest]},
            device_id_type=MESH,
        )

    def span(lo, hi):
        return pl.ds(lo, hi - lo)

    full4 = pl.ds(0, 4)
    both = pl.ds(0, 2)

    def build(k):
        def msg(number, where, dest):
            return (number, message(k, number, where, dest))

        a, b = span(A0, A1), span(B0, B1)
        c1, c2, c = span(C10, C11), span(C20, C21), span(C10, C21)
        direct1 = [
            msg(1, (y, z, x, c1), "xp"),
            msg(2, (y, z, x, c1), "xm"),
            msg(5, (y, z, x, c2), "zp"),
            msg(6, (y, z, x, c2), "zm"),
            msg(0, (y, z, x, span(A0, B1)), "y"),
        ]
        fwd1 = [
            (1, msg(3, (y, z, xm, span(C10, C1M)), "xp")),
            (2, msg(4, (y, z, xp, span(C1M, C11)), "xm")),
            (5, msg(7, (y, zm, x, span(C20, C2M)), "zp")),
            (6, msg(8, (y, zp, x, span(C2M, C21)), "zm")),
        ]
        rest1 = [0, 3, 4, 7, 8]
        direct2 = [
            msg(9, (both, z, x, a), "xp"),
            msg(10, (both, z, x, a), "xm"),
            msg(13, (both, z, x, b), "zp"),
            msg(14, (both, z, x, b), "zm"),
            msg(17, (y, z, full4, c1), "zp"),
            msg(18, (y, z, full4, c1), "zm"),
            msg(21, (y, full4, x, c2), "xp"),
            msg(22, (y, full4, x, c2), "xm"),
        ]
        lo2, hi2 = pl.ds(0, 2), pl.ds(2, 2)
        fwd2 = [
            (9, msg(11, (0, z, xm, a), "xp")),
            (10, msg(12, (1, z, xp, a), "xm")),
            (13, msg(15, (0, zm, x, b), "zp")),
            (14, msg(16, (1, zp, x, b), "zm")),
            (17, msg(19, (y, zm, lo2, c1), "zp")),
            (18, msg(20, (y, zp, hi2, c1), "zm")),
            (21, msg(23, (y, lo2, xm, c2), "xp")),
            (22, msg(24, (y, hi2, xp, c2), "xm")),
        ]
        rest2 = [11, 12, 15, 16, 19, 20, 23, 24]
        direct3 = [
            msg(25, (0, z, full4, a), "zp"),
            msg(27, (1, z, full4, a), "zm"),
            msg(31, (0, full4, x, b), "xp"),
            msg(33, (1, full4, x, b), "xm"),
            msg(37, (y, full4, full4, c), "y"),
            msg(26, (1, z, full4, a), "zp"),
            msg(28, (0, z, full4, a), "zm"),
            msg(32, (1, full4, x, b), "xp"),
            msg(34, (0, full4, x, b), "xm"),
        ]
        fwd3 = [
            (25, msg(29, (0, zm, full4, a), "zp")),
            (27, msg(30, (1, zp, full4, a), "zm")),
            (31, msg(35, (0, full4, xm, b), "xp")),
            (33, msg(36, (1, full4, xp, b), "xm")),
        ]
        rest3 = [26, 28, 32, 34, 29, 30, 35, 36, 37]
        return {1: (direct1, fwd1, rest1), 2: (direct2, fwd2, rest2), 3: (direct3, fwd3, rest3)}

    plan = [build(k) for k in range(4)]
    by_number = []
    for k in range(4):
        found = {}
        for step in (1, 2, 3):
            direct, fwd, rest = plan[k][step]
            for number, copy in direct:
                found[number] = copy
            for unused, (number, copy) in fwd:
                found[number] = copy
        by_number.append(found)

    def direct(step, k):
        for unused, copy in plan[k][step][0]:
            copy.start()

    def forward(step, k):
        for arrived, (unused, copy) in plan[k][step][1]:
            by_number[k][arrived].wait_recv()
            copy.start()

    def finish(step, k):
        for number in plan[k][step][2]:
            by_number[k][number].wait_recv()

    def transform(k, store):
        table_copies[k].wait()
        if k == 0:
            for copy in table_copies[1:]:
                copy.start()
        spectra = jnp.dot(filtered[...], tab[k], preferred_element_type=F32).astype(BF)
        for m in range(2):
            for t in range(FR_DEV):
                for p in range(2):
                    column = (m * 2 + p) * BLOCK_CH
                    store(
                        m * 16 + t * 2 + p,
                        spectra[t * STN_DEV : (t + 1) * STN_DEV, column : column + BLOCK_CH],
                    )

    def store_own(unit, value):
        grp[0][y, z, x, unit] = value

    for dest in range(GROUPS):
        place = (dest // 16, (dest // 4) % 4, dest % 4)
        to_send[place + (0,)] = lists[dest]
        to_send[place + (1,)] = jnp.concatenate(
            [jnp.broadcast_to(facts[i : i + 1], (8, BLOCK_CH)) for i in (dest * 2, dest * 2 + 1)],
            axis=0,
        ).astype(BF)

    def route(number, source, target, device):
        return pltpu.make_async_remote_copy(
            src_ref=source,
            dst_ref=target,
            send_sem=route_send.at[number],
            recv_sem=route_recv.at[number],
            device_id={"stn": device},
            device_id_type=MESH,
        )

    pl.semaphore_wait(barrier, 10)
    route_y = route(0, to_send.at[yn], by_y.at[y], to["y"])
    route_y.start()
    keep_y = pltpu.make_async_copy(to_send.at[y], by_y.at[y], own_sem.at[0])
    keep_y.start()
    exchange = []

    def exchange_out(k):
        def store_held(unit, value):
            held[k - 1, unit] = value

        transform(k, store_held)
        copy = pltpu.make_async_remote_copy(
            src_ref=held.at[k - 1],
            dst_ref=grp[4 - k].at[y, z, x],
            send_sem=a2a_send.at[k],
            recv_sem=a2a_recv.at[k],
            device_id={"tm": chunk[k]},
            device_id_type=MESH,
        )
        copy.start()
        exchange.append(copy)

    def exchanged(k):
        pltpu.make_async_remote_copy(
            src_ref=held.at[0],
            dst_ref=grp[k].at[y, z, x],
            send_sem=a2a_send.at[4 - k],
            recv_sem=a2a_recv.at[4 - k],
            device_id={"tm": chunk[k]},
            device_id_type=MESH,
        ).wait_recv()

    def correlate(k, first, last):
        def slot(s, carry):
            g = s // MOST
            partner = jnp.clip(info[s, 1], 0, GROUPS - 1)
            m = jnp.clip(info[s, 2], 0, 1)
            units = pl.ds(m * 16, 16)
            own = grp[k][g // 16, (g // 4) % 4, g % 4, units]
            rows32[...] = own.reshape(256, BLOCK_CH).astype(F32)
            other = grp[k][partner // 16, (partner // 4) % 4, partner % 4, units]
            for a in range(STN_DEV):
                real, imag = [], []
                for t in range(FR_DEV):
                    r = t * 32 + a
                    a_r = jnp.broadcast_to(rows32[r : r + 1, :], (STN_DEV, BLOCK_CH)).astype(BF)
                    a_i = jnp.broadcast_to(
                        rows32[r + 16 : r + 17, :], (STN_DEV, BLOCK_CH)
                    ).astype(BF)
                    b_r, b_i = other[2 * t], other[2 * t + 1]
                    real += [a_r * b_r + a_i * b_i]
                    imag += [a_i * b_r - a_r * b_i]
                while len(real) > 1:
                    real = [real[i] + real[i + 1] for i in range(0, len(real), 2)]
                    imag = [imag[i] + imag[i + 1] for i in range(0, len(imag), 2)]
                rows = slice(a * STN_DEV, (a + 1) * STN_DEV)
                if k == 0:
                    vis[s, rows, :BLOCK_CH] = real[0]
                    vis[s, rows, BLOCK_CH:] = imag[0]
                else:
                    vis[s, rows, :BLOCK_CH] = vis[s, rows, :BLOCK_CH] + real[0]
                    vis[s, rows, BLOCK_CH:] = vis[s, rows, BLOCK_CH:] + imag[0]
            return carry

        lax.fori_loop(first, last, slot, 0)

    transform(0, store_own)
    direct(1, 0)
    keep_y.wait()
    route_y.wait_recv()
    routes_z = [
        route(i, by_y.at[:, (z + i) % 4], by_z.at[z], along_z[i]) for i in range(1, 4)
    ]
    for copy in routes_z:
        copy.start()
    keep_z = pltpu.make_async_copy(by_y.at[:, z], by_z.at[z], own_sem.at[1])
    keep_z.start()
    exchange_out(1)
    forward(1, 0)
    exchange_out(2)
    finish(1, 0)
    direct(2, 0)
    keep_z.wait()
    for copy in routes_z:
        copy.wait_recv()
    routes_x = [
        route(3 + i, by_z.at[:, :, (x + i) % 4], by_x.at[x], along_x[i]) for i in range(1, 4)
    ]
    for copy in routes_x:
        copy.start()
    keep_x = pltpu.make_async_copy(by_z.at[:, :, x], by_x.at[x], own_sem.at[2])
    keep_x.start()
    exchange_out(3)
    forward(2, 0)
    exchanged(1)
    direct(1, 1)
    exchanged(2)
    direct(1, 2)
    forward(1, 1)
    finish(1, 1)
    direct(2, 1)
    finish(2, 0)
    direct(3, 0)
    exchanged(3)
    direct(1, 3)
    forward(1, 2)
    forward(1, 3)
    keep_x.wait()
    for copy in routes_x:
        copy.wait_recv()
    for g in range(GROUPS):
        unit = by_x[g % 4, (g // 4) % 4, g // 16, 1].astype(F32).astype(jnp.int32)
        facts_all[2 * g : 2 * g + 1] = unit[0:1]
        facts_all[2 * g + 1 : 2 * g + 2] = unit[8:9]
    to_scalars = pltpu.make_async_copy(facts_all, info, own_sem.at[3])
    to_scalars.start()
    to_next = pltpu.make_async_copy(facts_all, out_facts, own_sem.at[4])
    to_next.start()
    lists_next = pltpu.make_async_copy(by_x, out_lists, own_sem.at[5])
    lists_next.start()
    to_scalars.wait()
    forward(2, 1)
    half = SLOTS // 2
    for k in range(4):
        if k < 2:
            finish(1, k + 2)
            direct(2, k + 2)
        forward(3, k)
        if k > 0:
            correlate(k - 1, half, SLOTS)
        if k < 3:
            finish(2, k + 1)
            direct(3, k + 1)
        if k < 2:
            forward(2, k + 2)
        finish(3, k)
        if k < 3:
            correlate(k, 0, half)
    copies = []
    for i in range(4):
        part = pl.ds(i * (SLOTS // 4), SLOTS // 4)
        correlate(3, i * (SLOTS // 4), (i + 1) * (SLOTS // 4))
        copy = pltpu.make_async_copy(vis.at[part], out.at[part], out_sem.at[i])
        copy.start()
        copies.append(copy)
    for k in range(4):
        for number in range(MESSAGES):
            by_number[k][number].wait_send()
    for copy in exchange:
        copy.wait_send()
    for copy in copies:
        copy.wait()
    for copy in [route_y] + routes_z + routes_x:
        copy.wait_send()
    to_next.wait()
    lists_next.wait()


def gather_and_correlate(lists, facts, filtered, table):
    vmem = pl.BlockSpec(memory_space=pltpu.VMEM)
    anywhere = pl.BlockSpec(memory_space=pl.ANY)
    return pl.pallas_call(
        gather_kernel,
        out_shape=(
            jax.ShapeDtypeStruct((SLOTS, ROWS, 2 * BLOCK_CH), BF),
            jax.ShapeDtypeStruct((4, 4, 2, 2, STN_DEV, BLOCK_CH), BF),
            jax.ShapeDtypeStruct((SLOTS, BLOCK_CH), jnp.int32),
        ),
        in_specs=[vmem, vmem, vmem, anywhere],
        out_specs=(anywhere, anywhere, anywhere),
        scratch_shapes=[
            *[pltpu.VMEM((2, 4, 4, UNITS, STN_DEV, BLOCK_CH), BF) for unused in range(4)],
            pltpu.VMEM((3, UNITS, STN_DEV, BLOCK_CH), BF),
            pltpu.VMEM((4, FRAME, 4 * BLOCK_CH), BF),
            pltpu.VMEM((256, BLOCK_CH), F32),
            pltpu.VMEM((SLOTS, ROWS, 2 * BLOCK_CH), BF),
            pltpu.VMEM((2, 4, 4, 2, STN_DEV, BLOCK_CH), BF),
            pltpu.VMEM((2, 4, 4, 2, STN_DEV, BLOCK_CH), BF),
            pltpu.VMEM((4, 2, 4, 2, STN_DEV, BLOCK_CH), BF),
            pltpu.VMEM((4, 4, 2, 2, STN_DEV, BLOCK_CH), BF),
            pltpu.VMEM((SLOTS, BLOCK_CH), jnp.int32),
            pltpu.SMEM((SLOTS, BLOCK_CH), jnp.int32),
            pltpu.SemaphoreType.DMA((4,)),
            pltpu.SemaphoreType.DMA((4,)),
            pltpu.SemaphoreType.DMA((4,)),
            pltpu.SemaphoreType.DMA((4, MESSAGES)),
            pltpu.SemaphoreType.DMA((4, MESSAGES)),
            pltpu.SemaphoreType.DMA((4,)),
            pltpu.SemaphoreType.DMA((8,)),
            pltpu.SemaphoreType.DMA((8,)),
            pltpu.SemaphoreType.DMA((6,)),
        ],
        compiler_params=pltpu.CompilerParams(
            collective_id=0, has_side_effects=True, vmem_limit_bytes=48 * 2**20
        ),
        name="gather_correlate",
    )(lists, facts, filtered, table)


BATCH = 4
BATCHES = SLOTS // BATCH + 2
PIECES = 4


def gridding_kernel(
    info, lists, kernel_t, vis, out, total, weights_a, weights_b, along, tiles, order, used, sems
):
    used[0] = 0
    used[1] = 0

    def clear(s, carry):
        order[s] = SLOTS
        return carry

    lax.fori_loop(0, 2 * SLOTS, clear, 0)

    def place(s, carry):
        @pl.when(info[s, 0] > 0)
        def _():
            m = info[s, 2]
            at = used[m]
            order[m * SLOTS + at] = s
            used[m] = at + 1

        return carry

    lax.fori_loop(0, SLOTS, place, 0)
    first = (used[0] + BATCH - 1) // BATCH
    batches = first + (used[1] + BATCH - 1) // BATCH

    def member(j, i):
        m = jnp.where(j >= first, 1, 0)
        at = (j - m * first) * BATCH + i
        present = (j < batches) & (at < used[m])
        s = order[m * SLOTS + jnp.where(present, at, 0)]
        s = jnp.where(present, s, 0)
        return present, s, jnp.where(present, info[s, 0], 0)

    def tile_copy(j, i, s):
        return pltpu.make_async_copy(
            vis.at[s], tiles.at[j, pl.ds(i * ROWS, ROWS)], sems.at[j]
        )

    def fetch(j, carry):
        for i in range(BATCH):
            present, s, unused_alive = member(j, i)

            @pl.when(present)
            def _():
                tile_copy(j, i, s).start()

            @pl.when(jnp.logical_not(present))
            def _():
                tiles[j, i * ROWS : (i + 1) * ROWS] = jnp.zeros((ROWS, 2 * BLOCK_CH), BF)

        return carry

    lax.fori_loop(0, batches, fetch, 0)
    total[...] = jnp.zeros_like(total)

    def fetched(j):
        for i in range(BATCH):
            present, unused_s, unused_alive = member(j, i)

            @pl.when(present)
            def _():
                tile_copy(j, i, 0).wait()

    def axis_weight(position, offset):
        chosen = jnp.zeros((8, ROWS), F32)
        for o in range(8):
            column = jnp.broadcast_to(kernel_t[:, o : o + 1], (8, ROWS))
            chosen = jnp.where(jnp.broadcast_to(offset == o, (8, ROWS)), column, chosen)
        reach = lax.broadcasted_iota(jnp.int32, (SIDE, ROWS), 0) - jnp.broadcast_to(
            position, (SIDE, ROWS)
        )
        placed = jnp.zeros((SIDE, ROWS), F32)
        for k in range(8):
            placed = jnp.where(
                reach == k, jnp.broadcast_to(chosen[k : k + 1], (SIDE, ROWS)), placed
            )
        return placed

    def build_axes(j):
        for i in range(BATCH):
            unused_present, s, alive = member(j, i)
            g = s // MOST
            unit = lists[g % 4, (g // 4) % 4, g // 16, 0].astype(F32).astype(jnp.int32)
            half = jnp.where(s % MOST == 0, unit[0:8], unit[8:16])
            rows = [
                jnp.concatenate([half[2 * q : 2 * q + 1], half[2 * q + 1 : 2 * q + 2]], axis=1)
                for q in range(4)
            ]
            along[i, 0] = axis_weight(rows[0], rows[2])
            along_y = axis_weight(rows[1], rows[3])
            live = lax.broadcasted_iota(jnp.int32, (SIDE, ROWS), 1) < alive
            along[i, 1] = jnp.where(live, along_y, 0.0)

    def build_rows(weights, first_v, last_v):
        for i in range(BATCH):
            along_x = along[i, 0]
            for v in range(first_v, last_v):
                weights[v * SIDE : (v + 1) * SIDE, i * ROWS : (i + 1) * ROWS] = (
                    along_x * jnp.broadcast_to(along[i, 1, v : v + 1], (SIDE, ROWS))
                ).astype(BF)

    def step(j, weights, following):
        m = jnp.where(j >= first, 1, 0)
        build_axes(j + 1)
        span = CELLS // PIECES
        for q in range(PIECES):
            cells = slice(q * span, (q + 1) * span)
            build_rows(following, q * SIDE // PIECES, (q + 1) * SIDE // PIECES)
            total[m, cells] += jnp.dot(weights[cells], tiles[j], preferred_element_type=F32)

    build_axes(0)
    build_rows(weights_a, 0, SIDE)

    def pair(i, carry):
        j = 2 * i
        fetched(j)
        step(j, weights_a, weights_b)

        @pl.when(j + 1 < batches)
        def _():
            fetched(j + 1)
            step(j + 1, weights_b, weights_a)

        return carry

    lax.fori_loop(0, (batches + 1) // 2, pair, 0)
    for m in range(2):
        out[:, m, :] = total[m] * (1.0 / 32.0)


def gridding(info, lists, kernel_t, vis):
    vmem = pl.BlockSpec(memory_space=pltpu.VMEM)
    return pl.pallas_call(
        gridding_kernel,
        out_shape=jax.ShapeDtypeStruct((CELLS, 2, 2 * BLOCK_CH), F32),
        in_specs=[
            pl.BlockSpec(memory_space=pltpu.SMEM),
            vmem,
            vmem,
            pl.BlockSpec(memory_space=pl.ANY),
        ],
        out_specs=vmem,
        scratch_shapes=[
            pltpu.VMEM((2, CELLS, 2 * BLOCK_CH), F32),
            pltpu.VMEM((CELLS, BATCH * ROWS), BF),
            pltpu.VMEM((CELLS, BATCH * ROWS), BF),
            pltpu.VMEM((BATCH, 2, SIDE, ROWS), F32),
            pltpu.VMEM((BATCHES, BATCH * ROWS, 2 * BLOCK_CH), BF),
            pltpu.SMEM((2 * SLOTS,), jnp.int32),
            pltpu.SMEM((2,), jnp.int32),
            pltpu.SemaphoreType.DMA((BATCHES,)),
        ],
        compiler_params=pltpu.CompilerParams(vmem_limit_bytes=56 * 2**20),
        name="gridding",
    )(info, lists, kernel_t, vis)


def polyphase(voltages, filter_taps):
    by_frame = jnp.transpose(voltages, (1, 0, 2))
    frames = by_frame.shape[0] - TAPS + 1
    filtered = jnp.zeros((frames,) + by_frame.shape[1:], F32)
    for tap in range(TAPS):
        filtered = filtered + filter_taps[tap][None, None, :] * by_frame[
            tap : tap + frames
        ].astype(F32)
    return filtered.astype(BF).reshape(frames * by_frame.shape[1], FRAME)


def route_lists(uv_corners, kernel_offsets, row_counts, grid_tiles):
    owners = grid_tiles[0, 0]
    tiles = owners.shape[0]
    tile_ids = jnp.arange(tiles, dtype=jnp.int32)
    partner = (lax.axis_index("stn") + tile_ids // 2) % GROUPS
    extra = jnp.stack([row_counts[0, 0], partner, tile_ids % 2], axis=1)
    extra = jnp.pad(extra, ((0, 0), (0, BLOCK_CH - 3)))
    packed = jnp.concatenate(
        [uv_corners[0, 0].reshape(tiles, 512), kernel_offsets[0, 0].reshape(tiles, 512), extra],
        axis=1,
    ).astype(BF)
    same = owners[:, None] == owners[None, :]
    earlier = tile_ids[None, :] < tile_ids[:, None]
    slot_of = jnp.sum((same & earlier).astype(jnp.int32), axis=1)
    target = owners * MOST + slot_of
    picker = (target[None, :] == jnp.arange(SLOTS, dtype=jnp.int32)[:, None]).astype(BF)
    send = jnp.dot(picker, packed, preferred_element_type=F32)
    lists = send[:, :LISTS].astype(BF).reshape(GROUPS, STN_DEV, BLOCK_CH)
    return lists, send[:, LISTS:]


def on_device(voltages, pfb_taps, grid_kernel, uv_corners, kernel_offsets, row_counts, grid_tiles):
    lists, facts = route_lists(uv_corners, kernel_offsets, row_counts, grid_tiles)
    filtered = polyphase(voltages[:, 0], pfb_taps)
    vis, slot_lists, info = gather_and_correlate(lists, facts, filtered, jnp.asarray(dft_table()))
    return gridding(info, slot_lists, grid_kernel.T, vis)[None]


def solution(mesh):
    return jax.shard_map(
        on_device,
        mesh=mesh,
        in_specs=(
            P("stn", "tm", None, None),
            P(),
            P(),
            P("stn", "tm", None, None, None),
            P("stn", "tm", None, None, None),
            P("stn", "tm", None),
            P("stn", "tm", None),
        ),
        out_specs=P("stn", None, "tm", None),
        check_vma=False,
    )
```

```python
import math

import jax
import jax.numpy as jnp
import ml_dtypes
import numpy as np
from jax import lax
from jax.experimental import pallas as pl
from jax.experimental.pallas import tpu as pltpu
from jax.sharding import PartitionSpec as P

CHANNELS = 1024
FRAME = 2048
TAPS = 4
FR_DEV = 8
STN_DEV = 16
BLOCK_CH = 128
ROWS = 256
SIDE = 32
CELLS = 1024
MOST = 2
GROUPS = 32
SLOTS = GROUPS * MOST
LISTS = 4 * ROWS
BF = jnp.bfloat16
F32 = jnp.float32
MESH = pl.DeviceIdType.MESH

UNITS = 32
A_ENDS = (11, 10, 11, 10)
B_END = 21
C1_CUT, C1_END = 24, 26
C2_CUT = 29
MESSAGES = 38


def dft_table():
    samples = np.arange(FRAME, dtype=np.int64)
    channels = np.arange(CHANNELS, dtype=np.int64)
    phase = (samples[:, None] * channels[None, :]) % FRAME
    angle = phase.astype(np.float32) * np.float32(2.0 * math.pi / FRAME)
    scale = np.float32(1.0 / math.sqrt(FRAME))
    parts = np.stack([np.cos(angle) * scale, -np.sin(angle) * scale], axis=1)
    parts = parts.reshape(FRAME, 2, 4, 2, BLOCK_CH).transpose(2, 0, 3, 1, 4)
    return parts.reshape(4, FRAME, 4 * BLOCK_CH).astype(ml_dtypes.bfloat16)


def gather_kernel(
    lists,
    facts,
    frames,
    taps,
    table,
    out,
    out_lists,
    out_facts,
    grp0,
    grp1,
    grp2,
    grp3,
    filtered,
    held,
    tab,
    rows32,
    vis,
    to_send,
    by_y,
    by_z,
    by_x,
    facts_all,
    info,
    tab_sem,
    a2a_send,
    a2a_recv,
    send_sem,
    recv_sem,
    out_sem,
    route_send,
    route_recv,
    own_sem,
):
    grp = (grp0, grp1, grp2, grp3)
    me_s = lax.axis_index("stn")
    me_t = lax.axis_index("tm")
    y, z, x = me_s // 16, (me_s // 4) % 4, me_s % 4
    xp, xm = (x + 1) % 4, (x + 3) % 4
    zp, zm = (z + 1) % 4, (z + 3) % 4
    yn = 1 - y

    def at(yy, zz, xx):
        return yy * 16 + zz * 4 + xx

    to = {
        "xp": at(y, z, xp),
        "xm": at(y, z, xm),
        "zp": at(y, zp, x),
        "zm": at(y, zm, x),
        "y": at(yn, z, x),
    }
    along_z = [at(y, (z + i) % 4, x) for i in range(4)]
    along_x = [at(y, z, (x + i) % 4) for i in range(4)]
    chunk = [(me_t + k) % 4 for k in range(4)]

    table_copies = [
        pltpu.make_async_copy(table.at[chunk[k]], tab.at[k], tab_sem.at[k]) for k in range(4)
    ]
    table_copies[0].start()

    barrier = pltpu.get_barrier_semaphore()
    for name in to:
        pl.semaphore_signal(barrier, inc=1, device_id={"stn": to[name]}, device_id_type=MESH)
    for far in (along_z[2], along_x[2]):
        pl.semaphore_signal(barrier, inc=1, device_id={"stn": far}, device_id_type=MESH)
    for k in range(1, 4):
        pl.semaphore_signal(barrier, inc=1, device_id={"tm": chunk[k]}, device_id_type=MESH)

    def message(k, number, where, dest):
        ref = grp[k].at[where]
        return pltpu.make_async_remote_copy(
            src_ref=ref,
            dst_ref=ref,
            send_sem=send_sem.at[k, number],
            recv_sem=recv_sem.at[k, number],
            device_id={"stn": to[dest]},
            device_id_type=MESH,
        )

    def span(lo, hi):
        return pl.ds(lo, hi - lo)

    full4 = pl.ds(0, 4)
    both = pl.ds(0, 2)

    def build(k):
        def msg(number, where, dest):
            return (number, message(k, number, where, dest))

        a, b = span(0, A_ENDS[k]), span(A_ENDS[k], B_END)
        c1, c2, c = span(B_END, C1_END), span(C1_END, UNITS), span(B_END, UNITS)
        direct1 = [
            msg(1, (y, z, x, c1), "xp"),
            msg(2, (y, z, x, c1), "xm"),
            msg(5, (y, z, x, c2), "zp"),
            msg(6, (y, z, x, c2), "zm"),
            msg(0, (y, z, x, span(0, B_END)), "y"),
        ]
        fwd1 = [
            (1, msg(3, (y, z, xm, span(B_END, C1_CUT)), "xp")),
            (2, msg(4, (y, z, xp, span(C1_CUT, C1_END)), "xm")),
            (5, msg(7, (y, zm, x, span(C1_END, C2_CUT)), "zp")),
            (6, msg(8, (y, zp, x, span(C2_CUT, UNITS)), "zm")),
        ]
        rest1 = [0, 3, 4, 7, 8]
        direct2 = [
            msg(9, (both, z, x, a), "xp"),
            msg(10, (both, z, x, a), "xm"),
            msg(13, (both, z, x, b), "zp"),
            msg(14, (both, z, x, b), "zm"),
            msg(17, (y, z, full4, c1), "zp"),
            msg(18, (y, z, full4, c1), "zm"),
            msg(21, (y, full4, x, c2), "xp"),
            msg(22, (y, full4, x, c2), "xm"),
        ]
        lo2, hi2 = pl.ds(0, 2), pl.ds(2, 2)
        fwd2 = [
            (9, msg(11, (0, z, xm, a), "xp")),
            (10, msg(12, (1, z, xp, a), "xm")),
            (13, msg(15, (0, zm, x, b), "zp")),
            (14, msg(16, (1, zp, x, b), "zm")),
            (17, msg(19, (y, zm, lo2, c1), "zp")),
            (18, msg(20, (y, zp, hi2, c1), "zm")),
            (21, msg(23, (y, lo2, xm, c2), "xp")),
            (22, msg(24, (y, hi2, xp, c2), "xm")),
        ]
        rest2 = [11, 12, 15, 16, 19, 20, 23, 24]
        direct3 = [
            msg(25, (0, z, full4, a), "zp"),
            msg(27, (1, z, full4, a), "zm"),
            msg(31, (0, full4, x, b), "xp"),
            msg(33, (1, full4, x, b), "xm"),
            msg(37, (y, full4, full4, c), "y"),
            msg(26, (1, z, full4, a), "zp"),
            msg(28, (0, z, full4, a), "zm"),
            msg(32, (1, full4, x, b), "xp"),
            msg(34, (0, full4, x, b), "xm"),
        ]
        fwd3 = [
            (25, msg(29, (0, zm, full4, a), "zp")),
            (27, msg(30, (1, zp, full4, a), "zm")),
            (31, msg(35, (0, full4, xm, b), "xp")),
            (33, msg(36, (1, full4, xp, b), "xm")),
        ]
        rest3 = [26, 28, 32, 34, 29, 30, 35, 36, 37]
        return {1: (direct1, fwd1, rest1), 2: (direct2, fwd2, rest2), 3: (direct3, fwd3, rest3)}

    plan = [build(k) for k in range(4)]
    by_number = []
    for k in range(4):
        found = {}
        for step in (1, 2, 3):
            direct, fwd, rest = plan[k][step]
            for number, copy in direct:
                found[number] = copy
            for unused, (number, copy) in fwd:
                found[number] = copy
        by_number.append(found)

    def direct(step, k):
        for unused, copy in plan[k][step][0]:
            copy.start()

    def forward(step, k):
        for arrived, (unused, copy) in plan[k][step][1]:
            by_number[k][arrived].wait_recv()
            copy.start()

    def finish(step, k):
        for number in plan[k][step][2]:
            by_number[k][number].wait_recv()

    def transform(k, store):
        table_copies[k].wait()
        if k == 0:
            for copy in table_copies[1:]:
                copy.start()
        spectra = jnp.dot(filtered[...], tab[k], preferred_element_type=F32).astype(BF)
        for m in range(2):
            for t in range(FR_DEV):
                for p in range(2):
                    column = (m * 2 + p) * BLOCK_CH
                    store(
                        m * 16 + t * 2 + p,
                        spectra[t * STN_DEV : (t + 1) * STN_DEV, column : column + BLOCK_CH],
                    )

    def store_own(unit, value):
        grp[0][y, z, x, unit] = value

    for dest in range(GROUPS):
        place = (dest // 16, (dest // 4) % 4, dest % 4)
        to_send[place + (0,)] = lists[dest]
        to_send[place + (1,)] = jnp.concatenate(
            [jnp.broadcast_to(facts[i : i + 1], (8, BLOCK_CH)) for i in (dest * 2, dest * 2 + 1)],
            axis=0,
        ).astype(BF)

    def route(number, source, target, device):
        return pltpu.make_async_remote_copy(
            src_ref=source,
            dst_ref=target,
            send_sem=route_send.at[number],
            recv_sem=route_recv.at[number],
            device_id={"stn": device},
            device_id_type=MESH,
        )

    for column in range(0, FRAME, 256):
        columns = slice(column, column + 256)
        samples = [frames[i, :, columns].astype(F32) for i in range(FR_DEV + TAPS - 1)]
        for t in range(FR_DEV):
            value = taps[0:1, columns] * samples[t]
            for tap in range(1, TAPS):
                value = value + taps[tap : tap + 1, columns] * samples[t + tap]
            filtered[t * STN_DEV : (t + 1) * STN_DEV, columns] = value.astype(BF)

    pl.semaphore_wait(barrier, 10)
    route_y = route(0, to_send.at[yn], by_y.at[y], to["y"])
    route_y.start()
    keep_y = pltpu.make_async_copy(to_send.at[y], by_y.at[y], own_sem.at[0])
    keep_y.start()
    exchange = []

    def exchange_out(k):
        def store_held(unit, value):
            held[k - 1, unit] = value

        transform(k, store_held)
        copy = pltpu.make_async_remote_copy(
            src_ref=held.at[k - 1],
            dst_ref=grp[4 - k].at[y, z, x],
            send_sem=a2a_send.at[k],
            recv_sem=a2a_recv.at[k],
            device_id={"tm": chunk[k]},
            device_id_type=MESH,
        )
        copy.start()
        exchange.append(copy)

    def exchanged(k):
        pltpu.make_async_remote_copy(
            src_ref=held.at[0],
            dst_ref=grp[k].at[y, z, x],
            send_sem=a2a_send.at[4 - k],
            recv_sem=a2a_recv.at[4 - k],
            device_id={"tm": chunk[k]},
            device_id_type=MESH,
        ).wait_recv()

    def correlate(k, first, last):
        def slot(s, carry):
            g = s // MOST
            partner = jnp.clip(info[s, 1], 0, GROUPS - 1)
            m = jnp.clip(info[s, 2], 0, 1)
            units = pl.ds(m * 16, 16)
            own = grp[k][g // 16, (g // 4) % 4, g % 4, units]
            rows32[...] = own.reshape(256, BLOCK_CH).astype(F32)
            other = grp[k][partner // 16, (partner // 4) % 4, partner % 4, units]
            for a in range(STN_DEV):
                real, imag = [], []
                for t in range(FR_DEV):
                    r = t * 32 + a
                    a_r = jnp.broadcast_to(rows32[r : r + 1, :], (STN_DEV, BLOCK_CH)).astype(BF)
                    a_i = jnp.broadcast_to(
                        rows32[r + 16 : r + 17, :], (STN_DEV, BLOCK_CH)
                    ).astype(BF)
                    b_r, b_i = other[2 * t], other[2 * t + 1]
                    real += [a_r * b_r + a_i * b_i]
                    imag += [a_i * b_r - a_r * b_i]
                while len(real) > 1:
                    real = [real[i] + real[i + 1] for i in range(0, len(real), 2)]
                    imag = [imag[i] + imag[i + 1] for i in range(0, len(imag), 2)]
                rows = slice(a * STN_DEV, (a + 1) * STN_DEV)
                if k == 0:
                    vis[s, rows, :BLOCK_CH] = real[0]
                    vis[s, rows, BLOCK_CH:] = imag[0]
                else:
                    vis[s, rows, :BLOCK_CH] = vis[s, rows, :BLOCK_CH] + real[0]
                    vis[s, rows, BLOCK_CH:] = vis[s, rows, BLOCK_CH:] + imag[0]
            return carry

        lax.fori_loop(first, last, slot, 0)

    transform(0, store_own)
    direct(1, 0)
    keep_y.wait()
    route_y.wait_recv()
    routes_z = [
        route(i, by_y.at[:, (z + i) % 4], by_z.at[z], along_z[i]) for i in range(1, 4)
    ]
    for copy in routes_z:
        copy.start()
    keep_z = pltpu.make_async_copy(by_y.at[:, z], by_z.at[z], own_sem.at[1])
    keep_z.start()
    exchange_out(1)
    forward(1, 0)
    exchange_out(2)
    finish(1, 0)
    direct(2, 0)
    keep_z.wait()
    for copy in routes_z:
        copy.wait_recv()
    routes_x = [
        route(3 + i, by_z.at[:, :, (x + i) % 4], by_x.at[x], along_x[i]) for i in range(1, 4)
    ]
    for copy in routes_x:
        copy.start()
    keep_x = pltpu.make_async_copy(by_z.at[:, :, x], by_x.at[x], own_sem.at[2])
    keep_x.start()
    exchange_out(3)
    forward(2, 0)
    exchanged(1)
    direct(1, 1)
    exchanged(2)
    direct(1, 2)
    forward(1, 1)
    finish(1, 1)
    direct(2, 1)
    finish(2, 0)
    direct(3, 0)
    exchanged(3)
    direct(1, 3)
    forward(1, 2)
    forward(1, 3)
    keep_x.wait()
    for copy in routes_x:
        copy.wait_recv()
    for g in range(GROUPS):
        unit = by_x[g % 4, (g // 4) % 4, g // 16, 1].astype(F32).astype(jnp.int32)
        facts_all[2 * g : 2 * g + 1] = unit[0:1]
        facts_all[2 * g + 1 : 2 * g + 2] = unit[8:9]
    to_scalars = pltpu.make_async_copy(facts_all, info, own_sem.at[3])
    to_scalars.start()
    to_next = pltpu.make_async_copy(facts_all, out_facts, own_sem.at[4])
    to_next.start()
    lists_next = pltpu.make_async_copy(by_x, out_lists, own_sem.at[5])
    lists_next.start()
    to_scalars.wait()
    forward(2, 1)
    half = SLOTS // 2
    for k in range(4):
        if k < 2:
            finish(1, k + 2)
            direct(2, k + 2)
        forward(3, k)
        if k > 0:
            correlate(k - 1, half, SLOTS)
        if k < 3:
            finish(2, k + 1)
            direct(3, k + 1)
        if k < 2:
            forward(2, k + 2)
        finish(3, k)
        if k < 3:
            correlate(k, 0, half)
    copies = []
    for i in range(4):
        part = pl.ds(i * (SLOTS // 4), SLOTS // 4)
        correlate(3, i * (SLOTS // 4), (i + 1) * (SLOTS // 4))
        copy = pltpu.make_async_copy(vis.at[part], out.at[part], out_sem.at[i])
        copy.start()
        copies.append(copy)
    for k in range(4):
        for number in range(MESSAGES):
            by_number[k][number].wait_send()
    for copy in exchange:
        copy.wait_send()
    for copy in copies:
        copy.wait()
    for copy in [route_y] + routes_z + routes_x:
        copy.wait_send()
    to_next.wait()
    lists_next.wait()


def gather_and_correlate(lists, facts, frames, taps, table):
    vmem = pl.BlockSpec(memory_space=pltpu.VMEM)
    anywhere = pl.BlockSpec(memory_space=pl.ANY)
    return pl.pallas_call(
        gather_kernel,
        out_shape=(
            jax.ShapeDtypeStruct((SLOTS, ROWS, 2 * BLOCK_CH), BF),
            jax.ShapeDtypeStruct((4, 4, 2, 2, STN_DEV, BLOCK_CH), BF),
            jax.ShapeDtypeStruct((SLOTS, BLOCK_CH), jnp.int32),
        ),
        in_specs=[vmem, vmem, vmem, vmem, anywhere],
        out_specs=(anywhere, anywhere, anywhere),
        scratch_shapes=[
            *[pltpu.VMEM((2, 4, 4, UNITS, STN_DEV, BLOCK_CH), BF) for unused in range(4)],
            pltpu.VMEM((FR_DEV * STN_DEV, FRAME), BF),
            pltpu.VMEM((3, UNITS, STN_DEV, BLOCK_CH), BF),
            pltpu.VMEM((4, FRAME, 4 * BLOCK_CH), BF),
            pltpu.VMEM((256, BLOCK_CH), F32),
            pltpu.VMEM((SLOTS, ROWS, 2 * BLOCK_CH), BF),
            pltpu.VMEM((2, 4, 4, 2, STN_DEV, BLOCK_CH), BF),
            pltpu.VMEM((2, 4, 4, 2, STN_DEV, BLOCK_CH), BF),
            pltpu.VMEM((4, 2, 4, 2, STN_DEV, BLOCK_CH), BF),
            pltpu.VMEM((4, 4, 2, 2, STN_DEV, BLOCK_CH), BF),
            pltpu.VMEM((SLOTS, BLOCK_CH), jnp.int32),
            pltpu.SMEM((SLOTS, BLOCK_CH), jnp.int32),
            pltpu.SemaphoreType.DMA((4,)),
            pltpu.SemaphoreType.DMA((4,)),
            pltpu.SemaphoreType.DMA((4,)),
            pltpu.SemaphoreType.DMA((4, MESSAGES)),
            pltpu.SemaphoreType.DMA((4, MESSAGES)),
            pltpu.SemaphoreType.DMA((4,)),
            pltpu.SemaphoreType.DMA((8,)),
            pltpu.SemaphoreType.DMA((8,)),
            pltpu.SemaphoreType.DMA((6,)),
        ],
        compiler_params=pltpu.CompilerParams(
            collective_id=0, has_side_effects=True, vmem_limit_bytes=48 * 2**20
        ),
        name="gather_correlate",
    )(lists, facts, frames, taps, table)


BATCH = 2
BATCHES = SLOTS // BATCH + 2
PIECES = 4


def gridding_kernel(
    info, lists, kernel, vis, out, kernel_t, total, weights_a, weights_b, along, tiles, order, used, sems
):
    used[0] = 0
    used[1] = 0

    def place(s, carry):
        @pl.when(info[s, 0] > 0)
        def _():
            m = info[s, 2]
            at = used[m]
            order[m * SLOTS + at] = s
            used[m] = at + 1

        return carry

    lax.fori_loop(0, SLOTS, place, 0)
    first = (used[0] + BATCH - 1) // BATCH
    batches = first + (used[1] + BATCH - 1) // BATCH

    def member(j, i):
        m = jnp.where(j >= first, 1, 0)
        at = (j - m * first) * BATCH + i
        present = (j < batches) & (at < used[m])
        s = jnp.where(present, order[m * SLOTS + jnp.where(present, at, 0)], 0)
        return present, s, jnp.where(present, info[s, 0], 0)

    def tile_copy(j, i, s):
        return pltpu.make_async_copy(
            vis.at[s], tiles.at[j, pl.ds(i * ROWS, ROWS)], sems.at[j]
        )

    def fetch(j, carry):
        for i in range(BATCH):
            present, s, unused_alive = member(j, i)

            @pl.when(present)
            def _():
                tile_copy(j, i, s).start()

            @pl.when(jnp.logical_not(present))
            def _():
                tiles[j, i * ROWS : (i + 1) * ROWS] = jnp.zeros((ROWS, 2 * BLOCK_CH), BF)

        return carry

    lax.fori_loop(0, batches, fetch, 0)
    total[...] = jnp.zeros_like(total)
    row = lax.broadcasted_iota(jnp.int32, (8, BLOCK_CH), 0)
    lane = lax.broadcasted_iota(jnp.int32, (8, BLOCK_CH), 1)
    transposed = jnp.zeros((8, BLOCK_CH), F32)
    for o in range(8):
        for k in range(8):
            transposed = jnp.where((row == k) & (lane == o), kernel[o, k], transposed)
    kernel_t[...] = transposed

    def fetched(j):
        for i in range(BATCH):
            present, unused_s, unused_alive = member(j, i)

            @pl.when(present)
            def _():
                tile_copy(j, i, 0).wait()

    def axis_weight(position, offset):
        chosen = jnp.zeros((8, ROWS), F32)
        for o in range(8):
            column = jnp.broadcast_to(kernel_t[:, o : o + 1], (8, ROWS))
            chosen = jnp.where(jnp.broadcast_to(offset == o, (8, ROWS)), column, chosen)
        reach = lax.broadcasted_iota(jnp.int32, (SIDE, ROWS), 0) - jnp.broadcast_to(
            position, (SIDE, ROWS)
        )
        placed = jnp.zeros((SIDE, ROWS), F32)
        for k in range(8):
            placed = jnp.where(
                reach == k, jnp.broadcast_to(chosen[k : k + 1], (SIDE, ROWS)), placed
            )
        return placed

    def build_axes(j):
        for i in range(BATCH):
            unused_present, s, alive = member(j, i)
            g = s // MOST
            unit = lists[g % 4, (g // 4) % 4, g // 16, 0].astype(F32).astype(jnp.int32)
            half = jnp.where(s % MOST == 0, unit[0:8], unit[8:16])
            rows = [
                jnp.concatenate([half[2 * q : 2 * q + 1], half[2 * q + 1 : 2 * q + 2]], axis=1)
                for q in range(4)
            ]
            along[i, 0] = axis_weight(rows[0], rows[2])
            along_y = axis_weight(rows[1], rows[3])
            live = lax.broadcasted_iota(jnp.int32, (SIDE, ROWS), 1) < alive
            along[i, 1] = jnp.where(live, along_y, 0.0)

    def build_rows(weights, first_v, last_v):
        for i in range(BATCH):
            along_x = along[i, 0]
            for v in range(first_v, last_v):
                weights[v * SIDE : (v + 1) * SIDE, i * ROWS : (i + 1) * ROWS] = (
                    along_x * jnp.broadcast_to(along[i, 1, v : v + 1], (SIDE, ROWS))
                ).astype(BF)

    def step(j, weights, following):
        m = jnp.where(j >= first, 1, 0)
        build_axes(j + 1)
        span = CELLS // PIECES
        for q in range(PIECES):
            cells = slice(q * span, (q + 1) * span)
            build_rows(following, q * SIDE // PIECES, (q + 1) * SIDE // PIECES)
            total[m, cells] += jnp.dot(weights[cells], tiles[j], preferred_element_type=F32)

    build_axes(0)
    build_rows(weights_a, 0, SIDE)

    def pair(i, carry):
        j = 2 * i
        fetched(j)
        step(j, weights_a, weights_b)

        @pl.when(j + 1 < batches)
        def _():
            fetched(j + 1)
            step(j + 1, weights_b, weights_a)

        return carry

    lax.fori_loop(0, (batches + 1) // 2, pair, 0)
    for m in range(2):
        out[:, m, :] = total[m] * (1.0 / 32.0)


def gridding(info, lists, kernel, vis):
    vmem = pl.BlockSpec(memory_space=pltpu.VMEM)
    return pl.pallas_call(
        gridding_kernel,
        out_shape=jax.ShapeDtypeStruct((CELLS, 2, 2 * BLOCK_CH), F32),
        in_specs=[
            pl.BlockSpec(memory_space=pltpu.SMEM),
            vmem,
            pl.BlockSpec(memory_space=pltpu.SMEM),
            pl.BlockSpec(memory_space=pl.ANY),
        ],
        out_specs=vmem,
        scratch_shapes=[
            pltpu.VMEM((8, BLOCK_CH), F32),
            pltpu.VMEM((2, CELLS, 2 * BLOCK_CH), F32),
            pltpu.VMEM((CELLS, BATCH * ROWS), BF),
            pltpu.VMEM((CELLS, BATCH * ROWS), BF),
            pltpu.VMEM((BATCH, 2, SIDE, ROWS), F32),
            pltpu.VMEM((BATCHES, BATCH * ROWS, 2 * BLOCK_CH), BF),
            pltpu.SMEM((2 * SLOTS,), jnp.int32),
            pltpu.SMEM((2,), jnp.int32),
            pltpu.SemaphoreType.DMA((BATCHES,)),
        ],
        compiler_params=pltpu.CompilerParams(vmem_limit_bytes=56 * 2**20),
        name="gridding",
    )(info, lists, kernel, vis)


def route_lists(uv_corners, kernel_offsets, row_counts, grid_tiles):
    owners = grid_tiles[0, 0]
    tiles = owners.shape[0]
    tile_ids = jnp.arange(tiles, dtype=jnp.int32)
    partner = (lax.axis_index("stn") + tile_ids // 2) % GROUPS
    extra = jnp.stack([row_counts[0, 0], partner, tile_ids % 2], axis=1)
    extra = jnp.pad(extra, ((0, 0), (0, BLOCK_CH - 3)))
    packed = jnp.concatenate(
        [uv_corners[0, 0].reshape(tiles, 512), kernel_offsets[0, 0].reshape(tiles, 512), extra],
        axis=1,
    ).astype(BF)
    same = owners[:, None] == owners[None, :]
    earlier = tile_ids[None, :] < tile_ids[:, None]
    slot_of = jnp.sum((same & earlier).astype(jnp.int32), axis=1)
    target = owners * MOST + slot_of
    picker = (target[None, :] == jnp.arange(SLOTS, dtype=jnp.int32)[:, None]).astype(BF)
    send = jnp.dot(picker, packed, preferred_element_type=F32)
    lists = send[:, :LISTS].astype(BF).reshape(GROUPS, STN_DEV, BLOCK_CH)
    return lists, send[:, LISTS:]


def on_device(voltages, pfb_taps, grid_kernel, uv_corners, kernel_offsets, row_counts, grid_tiles):
    lists, facts = route_lists(uv_corners, kernel_offsets, row_counts, grid_tiles)
    frames = jnp.transpose(voltages[:, 0], (1, 0, 2))
    vis, slot_lists, info = gather_and_correlate(
        lists, facts, frames, pfb_taps, jnp.asarray(dft_table())
    )
    return gridding(info, slot_lists, grid_kernel, vis)[None]


def solution(mesh):
    return jax.shard_map(
        on_device,
        mesh=mesh,
        in_specs=(
            P("stn", "tm", None, None),
            P(),
            P(),
            P("stn", "tm", None, None, None),
            P("stn", "tm", None, None, None),
            P("stn", "tm", None),
            P("stn", "tm", None),
        ),
        out_specs=P("stn", None, "tm", None),
        check_vma=False,
    )
```
